1024 devices in a mesh: sites: 1024 (over x, y, z, core).
Axes of the slice: x: 4, y: 8, z: 16, core: 2. Of those that a mesh axis runs over, the one named last changes fastest.
Arguments:
- coords: float32 [8, 1572864], P(None, 'sites'), may hold values from -6 to 6
- inv_scale: float32 [8], replicated, may hold values from 0.25 to 1
- noise_var: float32 [1572864], P('sites'), may hold values from 0.5 to 2
- solution: float32 [16, 1572864], P(None, 'sites'), may hold values from -6 to 6
- residual: float32 [16, 1572864], P(None, 'sites'), may hold values from -40 to 40
- direction: float32 [16, 1572864], P(None, 'sites'), may hold values from -40 to 40
Outputs:
- new_solution: float32 [16, 1572864], P(None, 'sites')
- new_residual: float32 [16, 1572864], P(None, 'sites')
- new_direction: float32 [16, 1572864], P(None, 'sites')
The draws below stay inside these ranges and needn't reach their ends.
All inputs are finite; a program needn't handle non-finite values.
Results may differ from the reference program's by a relative error of at most 0.0003.
Values sent between devices are 32-bit elements; how exact they have to be, the bound alone decides.
No kernel may reach another device: no remote copies, remote signals or barrier semaphores. Data moves between devices by JAX's collectives and lax.ppermute only.
A program may use at most 32 MiB of HBM per device.

```python
import math
import jax
import jax.numpy as jnp
from jax import lax

DIMS = 8
RHS = 16
SITES_DEV = 1536
ROUNDS = 3
TOTAL_SITES = 1572864
N_SITES = 1024


def draw_residual(key, part):
    key = jax.random.fold_in(key, 11)
    first, second = jax.random.split(key, 2)
    position = jnp.arange(TOTAL_SITES, dtype=jnp.float32) / TOTAL_SITES
    ramp = 1.0 + 2.0 * position
    rough = jnp.exp(jax.random.uniform(second, (RHS, TOTAL_SITES), jnp.float32, -0.7, 0.7))
    base = jax.random.normal(first, (RHS, TOTAL_SITES), jnp.float32)
    return jnp.clip(base * ramp[None, :] * rough, -40.0, 40.0)


def draw_direction(key, part):
    key = jax.random.fold_in(key, 23)
    first, second = jax.random.split(key, 2)
    position = jnp.arange(TOTAL_SITES, dtype=jnp.float32) / TOTAL_SITES
    ramp = 1.0 + 2.0 * position
    rough = jnp.exp(jax.random.uniform(second, (RHS, TOTAL_SITES), jnp.float32, -0.7, 0.7))
    base = jax.random.normal(first, (RHS, TOTAL_SITES), jnp.float32)
    return jnp.clip(base * ramp[None, :] * rough, -40.0, 40.0)


def levels(stream_key, extent, cuts, least, high):
    level, own = 1.0, jax.random.fold_in(stream_key, 6)
    for dim, blocks in cuts:
        steps = jnp.exp(jax.random.uniform(jax.random.fold_in(own, dim), (blocks,), jnp.float32, least / len(cuts), high / len(cuts)))
        level = level * jnp.repeat(steps, extent[dim] // blocks).reshape([-1 if axis == dim else 1 for axis in range(len(extent))])
    return level


def scatter_about(key, extent, width, reach, shards=(), kind=jnp.bfloat16):
    factor_of = levels(key, extent, shards, -0.22, 0.18) if shards else 1.0
    entries = jax.random.normal(key, extent, jnp.float32) * width * factor_of
    return jnp.minimum(jnp.maximum(entries, -reach), reach).astype(kind)


def setup_inputs(seed: int = 0) -> dict:
    splits = jax.random.split(jax.random.key(seed), 7)
    return {
        "coords": scatter_about(splits[0], (DIMS, TOTAL_SITES), 1.0, 6.0, ((1, 1024),), jnp.float32),
        "inv_scale": jnp.clip(jnp.exp(jax.random.uniform(splits[1], (DIMS,), jnp.float32, math.log(0.25), math.log(1.0))), 0.25, 1.0),
        "noise_var": jnp.clip(jnp.exp(math.log(2.0) - 1.3862944 * jax.random.uniform(splits[2], (TOTAL_SITES,), jnp.float32) ** levels(splits[2], (TOTAL_SITES,), ((0, 1024),), -0.2, 0.2)), 0.5, 2.0),
        "solution": scatter_about(splits[3], (RHS, TOTAL_SITES), 1.0, 6.0, ((1, 1024),), jnp.float32),
        "residual": draw_residual(jax.random.fold_in(splits[6], 71), 0),
        "direction": draw_direction(jax.random.fold_in(splits[6], 71), 0),
    }


def kernel_tile(left, right, inv_scale):
    left_scaled = left * inv_scale[:, None]
    right_scaled = right * inv_scale[:, None]
    left_norm = lax.optimization_barrier(jnp.sum(left_scaled * left_scaled, axis=0))
    right_norm = lax.optimization_barrier(jnp.sum(right_scaled * right_scaled, axis=0))
    cross = jnp.dot(left_scaled.T, right_scaled, precision=lax.Precision.HIGHEST)
    squared = jnp.maximum(left_norm[:, None] + right_norm[None, :] - 2.0 * cross, 0.0)
    scaled_dist = jnp.sqrt(5.0 * squared)
    return (1.0 + scaled_dist + scaled_dist * scaled_dist / 3.0) * jnp.exp(-scaled_dist)

def reference(coords, inv_scale, noise_var, solution, residual, direction):
    coord_blocks = coords.reshape(DIMS, N_SITES, SITES_DEV)
    dir_blocks = direction.reshape(RHS, N_SITES, SITES_DEV)

    def one_block(block_index):
        own_coords = coord_blocks[:, block_index]
        running = 2.0 * ROUNDS * jnp.dot(dir_blocks[:, block_index], kernel_tile(own_coords, own_coords, inv_scale).T, precision=lax.Precision.HIGHEST)
        for offset in range(1, ROUNDS + 1):
            for heading in (1, -1):
                partner = ((block_index + heading * offset) % N_SITES).astype(jnp.int32)
                values = kernel_tile(own_coords, coord_blocks[:, partner], inv_scale)
                running = running + jnp.dot(dir_blocks[:, partner], values.T, precision=lax.Precision.HIGHEST)
        return running
    pieces = lax.map(one_block, jnp.arange(N_SITES, dtype=jnp.int32))
    gp_image = jnp.moveaxis(pieces, 0, 1).reshape(RHS, TOTAL_SITES) + noise_var[None, :] * direction
    old_norm = lax.optimization_barrier(jnp.sum(residual * residual, axis=1))
    curvature = lax.optimization_barrier(jnp.sum(direction * gp_image, axis=1))
    step_size = old_norm / curvature
    new_solution = solution + step_size[:, None] * direction
    new_residual = residual - step_size[:, None] * gp_image
    new_norm = lax.optimization_barrier(jnp.sum(new_residual * new_residual, axis=1))
    new_direction = new_residual + (new_norm / old_norm)[:, None] * direction
    return (new_solution, new_residual, new_direction)
```

```python
import functools
import math

import jax
import jax.numpy as jnp
from jax import lax
from jax.experimental import pallas as pl
from jax.experimental.pallas import tpu as pltpu
from jax.sharding import Mesh, PartitionSpec as P

ROUNDS = 3
TILE = 256
AXES = ("hi", "lo")
VMEM_LIMIT = 40 * 1024 * 1024

LN2 = math.log(2.0)
COORD_SCALE = math.sqrt(5.0) / LN2
SCALE = LN2 * LN2 / 3.0
LINEAR = 3.0 / LN2
CONSTANT = 1.0 / SCALE
TINY = 1e-30

bf16 = jnp.bfloat16
f32 = jnp.float32


def split2(value):
    high = value.astype(bf16)
    return high, (value - high.astype(f32)).astype(bf16)


def split3(value):
    high = value.astype(bf16).astype(f32)
    rest = value - high
    middle = rest.astype(bf16).astype(f32)
    low = (rest - middle).astype(bf16).astype(f32)
    return high, middle, low


def stacked(value):
    return jnp.concatenate(split2(value), axis=0)


def features(scaled, left):
    high, middle, low = split3(-2.0 * scaled if left else scaled)
    norm = split3(jnp.sum(scaled * scaled, axis=0, keepdims=True))
    row = lax.broadcasted_iota(jnp.int32, scaled.shape, 0)
    first = 0 if left else 3
    extra = jnp.where((row >= 3 - first) & (row < 6 - first), 1.0, 0.0)
    for place, part in enumerate(norm):
        extra = jnp.where(row == first + place, part, extra)
    zero = jnp.zeros_like(extra)
    if left:
        pieces = (high, high, middle, high, middle, low, extra, zero)
    else:
        pieces = (high, middle, high, low, middle, high, extra, zero)
    return jnp.concatenate(pieces, axis=0)


def covariance(squared):
    squared = jnp.maximum(squared, TINY)
    dist = squared * lax.rsqrt(squared)
    return ((dist + LINEAR) * dist + CONSTANT) * jnp.exp2(-dist)


def product(left, right):
    return jnp.dot(left, right, preferred_element_type=f32)


def product_t(left, right):
    return lax.dot_general(left, right, (((1,), (1,)), ((), ())), preferred_element_type=f32)


def applied(dot, sides, high, low):
    rows = sides.shape[0] // 2
    both = dot(sides, high)
    return both[:rows] + both[rows:] + dot(sides[:rows], low)


def prepare_body(coords_ref, inv_ref, dir_ref, packed_ref, left_ref, sides_ref):
    scaled = coords_ref[...] * (inv_ref[...] * COORD_SCALE)
    weighted = dir_ref[...] * SCALE
    packed_ref[0:8, :] = scaled
    packed_ref[8:24, :] = weighted
    left_ref[...] = features(scaled, True).T.astype(bf16)
    sides_ref[...] = stacked(weighted)


def pair_body(left_ref, sides_ref, far_ref, near_ref, back_ref):
    sites = far_ref.shape[1]
    right = features(far_ref[0:8, :], False).astype(bf16)
    far_sides = stacked(far_ref[8:24, :])
    near = None
    for start in range(0, sites, TILE):
        columns = slice(start, start + TILE)
        values = covariance(product(left_ref[...], right[:, columns]))
        high, low = split2(values)
        part = applied(product_t, far_sides[:, columns], high, low)
        near = part if near is None else near + part
        back_ref[:, columns] = applied(product, sides_ref[...], high, low)
    near_ref[...] = near


def self_body(left_ref, sides_ref, own_ref, out_ref):
    sites = own_ref.shape[1]
    right = features(own_ref[0:8, :], False).astype(bf16)
    out_ref[...] = jnp.zeros_like(out_ref)
    for start in range(0, sites, TILE):
        stop = start + TILE
        columns = slice(start, stop)
        values = covariance(product(left_ref[0:stop, :], right[:, columns]))
        high, low = split2(values)
        out_ref[:, 0:stop] += applied(product_t, sides_ref[:, columns], high, low)
        if start:
            out_ref[:, columns] += applied(product, sides_ref[:, 0:start], high[0:start], low[0:start])


def call(body, name, shapes, cost):
    return pl.pallas_call(
        body,
        out_shape=shapes,
        compiler_params=pltpu.CompilerParams(vmem_limit_bytes=VMEM_LIMIT),
        cost_estimate=pl.CostEstimate(flops=cost, bytes_accessed=600000, transcendentals=0),
        name=name,
    )


def shape(rows, columns, dtype=f32):
    return jax.ShapeDtypeStruct((rows, columns), dtype)


def prepare(coords, inv_scale, direction):
    sites, rhs = coords.shape[1], direction.shape[0]
    shapes = (shape(8 + rhs, sites), shape(sites, 64, bf16), shape(2 * rhs, sites, bf16))
    return call(prepare_body, "prepare", shapes, 10**7)(coords, inv_scale[:, None], direction)


def pair(left, sides, far):
    out = shape(16, far.shape[1])
    return call(pair_body, "pair", (out, out), 6 * 10**9)(left, sides, far)


def own_block(left, sides, packed):
    return call(self_body, "own", shape(16, packed.shape[1]), 4 * 10**9)(left, sides, packed)


def shifted(value, steps):
    count = lax.axis_size(AXES)
    pairs = [(source, (source + steps) % count) for source in range(count)]
    return lax.ppermute(value, AXES, pairs)


def total(values):
    for axis in ("lo", "hi"):
        count = lax.axis_size(axis)
        copies = jnp.broadcast_to(values[None], (count,) + values.shape)
        values = jnp.sum(lax.all_to_all(copies, axis, 0, 0, tiled=True), axis=0)
    return values


def local(coords, inv_scale, noise_var, solution, residual, direction):
    rhs = direction.shape[0]
    packed, left, sides = prepare(coords, inv_scale, direction)
    gp_image = noise_var[None, :] * direction
    fars = [shifted(packed, offset) for offset in range(1, ROUNDS + 1)]
    returns = []
    for offset, far in zip(range(1, ROUNDS + 1), fars):
        near, back = pair(left, sides, far)
        gp_image = gp_image + near
        returns.append(shifted(back, -offset))
    own = own_block(left, sides, packed)
    gp_image = gp_image + (2.0 * ROUNDS) * own
    for back in returns:
        gp_image = gp_image + back
    sums = [
        jnp.sum(residual * residual, axis=1),
        jnp.sum(direction * gp_image, axis=1),
        jnp.sum(residual * gp_image, axis=1),
        jnp.sum(gp_image * gp_image, axis=1),
    ]
    sums = total(jnp.concatenate(sums)).reshape(4, rhs)
    old_norm, curvature, mixed, image_norm = sums[0], sums[1], sums[2], sums[3]
    step_size = old_norm / curvature
    new_norm = jnp.maximum(old_norm + step_size * (step_size * image_norm - 2.0 * mixed), 0.0)
    new_solution = solution + step_size[:, None] * direction
    new_residual = residual - step_size[:, None] * gp_image
    new_direction = new_residual + (new_norm / old_norm)[:, None] * direction
    return (new_solution, new_residual, new_direction)


def solution(mesh):
    devices = mesh.devices.reshape(-1)
    low = 32
    split = Mesh(devices.reshape(devices.size // low, low), AXES)
    columns = P(None, AXES)
    return jax.shard_map(
        local,
        mesh=split,
        in_specs=(columns, P(), P(AXES), columns, columns, columns),
        out_specs=(columns, columns, columns),
        check_vma=False,
    )
```

```python
import functools
import math

import jax
import jax.numpy as jnp
from jax import lax
from jax.experimental import pallas as pl
from jax.experimental.pallas import tpu as pltpu
from jax.sharding import Mesh, PartitionSpec as P

ROUNDS = 3
TILE = 256
AXES = ("hi", "lo")
VMEM_LIMIT = 40 * 1024 * 1024

LN2 = math.log(2.0)
COORD_SCALE = math.sqrt(5.0) / LN2
SCALE = LN2 * LN2 / 3.0
LINEAR = 3.0 / LN2
CONSTANT = 1.0 / SCALE
TINY = 1e-30

bf16 = jnp.bfloat16
f32 = jnp.float32


def split2(value):
    high = value.astype(bf16)
    return high, (value - high.astype(f32)).astype(bf16)


def split3(value):
    high = value.astype(bf16).astype(f32)
    rest = value - high
    middle = rest.astype(bf16).astype(f32)
    low = (rest - middle).astype(bf16).astype(f32)
    return high, middle, low


def stacked(value):
    return jnp.concatenate(split2(value), axis=0)


def features(scaled, left):
    high, middle, low = split3(-2.0 * scaled if left else scaled)
    norm = split3(jnp.sum(scaled * scaled, axis=0, keepdims=True))
    row = lax.broadcasted_iota(jnp.int32, scaled.shape, 0)
    first = 0 if left else 3
    extra = jnp.where((row >= 3 - first) & (row < 6 - first), 1.0, 0.0)
    for place, part in enumerate(norm):
        extra = jnp.where(row == first + place, part, extra)
    zero = jnp.zeros_like(extra)
    if left:
        pieces = (high, high, middle, high, middle, low, extra, zero)
    else:
        pieces = (high, middle, high, low, middle, high, extra, zero)
    return jnp.concatenate(pieces, axis=0)


def covariance(squared):
    squared = jnp.maximum(squared, TINY)
    dist = squared * lax.rsqrt(squared)
    return ((dist + LINEAR) * dist + CONSTANT) * jnp.exp2(-dist)


def product(left, right):
    return jnp.dot(left, right, preferred_element_type=f32)


def product_t(left, right):
    return lax.dot_general(left, right, (((1,), (1,)), ((), ())), preferred_element_type=f32)


def applied(dot, sides, high, low):
    rows = sides.shape[0] // 2
    both = dot(sides, high)
    return both[:rows] + both[rows:] + dot(sides[:rows], low)


def prepare_body(packed_ref, left_ref, sides_ref):
    left_ref[...] = features(packed_ref[0:8, :], True).T.astype(bf16)
    sides_ref[...] = stacked(packed_ref[8:24, :])


def pairs_body(count, left_ref, sides_ref, *refs):
    fars, near_ref, back_ref = refs[:count], refs[count], refs[count + 1]
    near = None
    for place, far_ref in enumerate(fars):
        sites = far_ref.shape[1]
        rows = slice(16 * place, 16 * place + 16)
        right = features(far_ref[0:8, :], False).astype(bf16)
        far_sides = stacked(far_ref[8:24, :])
        for start in range(0, sites, TILE):
            columns = slice(start, start + TILE)
            values = covariance(product(left_ref[...], right[:, columns]))
            high, low = split2(values)
            part = applied(product_t, far_sides[:, columns], high, low)
            near = part if near is None else near + part
            back_ref[rows, columns] = applied(product, sides_ref[...], high, low)
    near_ref[...] = near


def self_body(left_ref, sides_ref, own_ref, out_ref):
    sites = own_ref.shape[1]
    right = features(own_ref[0:8, :], False).astype(bf16)
    out_ref[...] = jnp.zeros_like(out_ref)
    for start in range(0, sites, TILE):
        stop = start + TILE
        columns = slice(start, stop)
        values = covariance(product(left_ref[0:stop, :], right[:, columns]))
        high, low = split2(values)
        out_ref[:, 0:stop] += applied(product_t, sides_ref[:, columns], high, low)
        if start:
            out_ref[:, columns] += applied(product, sides_ref[:, 0:start], high[0:start], low[0:start])


def call(body, name, shapes, cost):
    return pl.pallas_call(
        body,
        out_shape=shapes,
        compiler_params=pltpu.CompilerParams(vmem_limit_bytes=VMEM_LIMIT),
        cost_estimate=pl.CostEstimate(flops=cost, bytes_accessed=600000, transcendentals=0),
        name=name,
    )


def shape(rows, columns, dtype=f32):
    return jax.ShapeDtypeStruct((rows, columns), dtype)


def prepare(packed):
    rows, sites = packed.shape
    shapes = (shape(sites, 64, bf16), shape(2 * (rows - 8), sites, bf16))
    return call(prepare_body, "prepare", shapes, 10**7)(packed)


def pairs(left, sides, fars):
    count, sites = len(fars), fars[0].shape[1]
    body = functools.partial(pairs_body, count)
    shapes = (shape(16, sites), shape(16 * count, sites))
    return call(body, "pairs%d" % count, shapes, 6 * count * 10**9)(left, sides, *fars)


def own_block(left, sides, packed):
    return call(self_body, "own", shape(16, packed.shape[1]), 4 * 10**9)(left, sides, packed)


def shifted(value, steps):
    count = lax.axis_size(AXES)
    pairs = [(source, (source + steps) % count) for source in range(count)]
    return lax.ppermute(value, AXES, pairs)


def total(values):
    for axis in ("lo", "hi"):
        count = lax.axis_size(axis)
        copies = jnp.broadcast_to(values[None], (count,) + values.shape)
        values = jnp.sum(lax.all_to_all(copies, axis, 0, 0, tiled=True), axis=0)
    return values


def local(coords, inv_scale, noise_var, solution, residual, direction):
    rhs = direction.shape[0]
    scaled = coords * (inv_scale * COORD_SCALE)[:, None]
    packed = jnp.concatenate([scaled, direction * SCALE], axis=0)
    left, sides = prepare(packed)
    gp_image = noise_var[None, :] * direction
    second = shifted(packed, 2)
    third = shifted(packed, 3)
    first = shifted(packed, 1)
    near, back = pairs(left, sides, [second, third])
    arrived = shifted(back, -2)
    near_first, back_first = pairs(left, sides, [first])
    returned = shifted(back_first + arrived[rhs:], -1)
    own = own_block(left, sides, packed)
    gp_image = gp_image + near + near_first + (2.0 * ROUNDS) * own + arrived[:rhs] + returned
    sums = [
        jnp.sum(residual * residual, axis=1),
        jnp.sum(direction * gp_image, axis=1),
        jnp.sum(residual * gp_image, axis=1),
        jnp.sum(gp_image * gp_image, axis=1),
    ]
    sums = total(jnp.concatenate(sums)).reshape(4, rhs)
    old_norm, curvature, mixed, image_norm = sums[0], sums[1], sums[2], sums[3]
    step_size = old_norm / curvature
    new_norm = jnp.maximum(old_norm + step_size * (step_size * image_norm - 2.0 * mixed), 0.0)
    new_solution = solution + step_size[:, None] * direction
    new_residual = residual - step_size[:, None] * gp_image
    new_direction = new_residual + (new_norm / old_norm)[:, None] * direction
    return (new_solution, new_residual, new_direction)


def solution(mesh):
    devices = mesh.devices.reshape(-1)
    low = 32
    split = Mesh(devices.reshape(devices.size // low, low), AXES)
    columns = P(None, AXES)
    return jax.shard_map(
        local,
        mesh=split,
        in_specs=(columns, P(), P(AXES), columns, columns, columns),
        out_specs=(columns, columns, columns),
        check_vma=False,
    )
```

```python
import functools
import math

import jax
import jax.numpy as jnp
from jax import lax
from jax.experimental import pallas as pl
from jax.experimental.pallas import tpu as pltpu
from jax.sharding import Mesh, PartitionSpec as P

ROUNDS = 3
TILE = 256
AXES = ("hi", "lo")
VMEM_LIMIT = 40 * 1024 * 1024

LN2 = math.log(2.0)
COORD_SCALE = math.sqrt(5.0) / LN2
SCALE = LN2 * LN2 / 3.0
LINEAR = 3.0 / LN2
CONSTANT = 1.0 / SCALE
TINY = 1e-30

bf16 = jnp.bfloat16
f32 = jnp.float32


def split2(value):
    high = value.astype(bf16)
    return high, (value - high.astype(f32)).astype(bf16)


def split3(value):
    high = value.astype(bf16).astype(f32)
    rest = value - high
    middle = rest.astype(bf16).astype(f32)
    low = (rest - middle).astype(bf16).astype(f32)
    return high, middle, low


def stacked(value):
    return jnp.concatenate(split2(value), axis=0)


def features(scaled, left):
    high, middle, low = split3(-2.0 * scaled if left else scaled)
    norm = split3(jnp.sum(scaled * scaled, axis=0, keepdims=True))
    row = lax.broadcasted_iota(jnp.int32, scaled.shape, 0)
    first = 0 if left else 3
    extra = jnp.where((row >= 3 - first) & (row < 6 - first), 1.0, 0.0)
    for place, part in enumerate(norm):
        extra = jnp.where(row == first + place, part, extra)
    zero = jnp.zeros_like(extra)
    if left:
        pieces = (high, high, middle, high, middle, low, extra, zero)
    else:
        pieces = (high, middle, high, low, middle, high, extra, zero)
    return jnp.concatenate(pieces, axis=0)


def covariance(squared):
    squared = jnp.maximum(squared, TINY)
    dist = squared * lax.rsqrt(squared)
    return ((dist + LINEAR) * dist + CONSTANT) * jnp.exp2(-dist)


def product(left, right):
    return jnp.dot(left, right, preferred_element_type=f32)


def product_t(left, right):
    return lax.dot_general(left, right, (((1,), (1,)), ((), ())), preferred_element_type=f32)


def applied(dot, sides, high, low):
    rows = sides.shape[0] // 2
    both = dot(sides, high)
    return both[:rows] + both[rows:] + dot(sides[:rows], low)


def prepare_body(packed_ref, left_ref, sides_ref):
    left_ref[...] = features(packed_ref[0:8, :], True).T.astype(bf16)
    sides_ref[...] = stacked(packed_ref[8:24, :])


def pairs_body(count, left_ref, sides_ref, *refs):
    fars, near_ref, back_ref = refs[:count], refs[count], refs[count + 1]
    near = None
    for place, far_ref in enumerate(fars):
        sites = far_ref.shape[1]
        rows = slice(16 * place, 16 * place + 16)
        right = features(far_ref[0:8, :], False).astype(bf16)
        far_sides = stacked(far_ref[8:24, :])
        for start in range(0, sites, TILE):
            columns = slice(start, start + TILE)
            values = covariance(product(left_ref[...], right[:, columns]))
            high, low = split2(values)
            part = applied(product_t, far_sides[:, columns], high, low)
            near = part if near is None else near + part
            back_ref[rows, columns] = applied(product, sides_ref[...], high, low)
    near_ref[...] = near


def self_body(left_ref, sides_ref, own_ref, out_ref):
    sites = own_ref.shape[1]
    right = features(own_ref[0:8, :], False).astype(bf16)
    out_ref[...] = jnp.zeros_like(out_ref)
    for start in range(0, sites, TILE):
        stop = start + TILE
        columns = slice(start, stop)
        values = covariance(product(left_ref[0:stop, :], right[:, columns]))
        high, low = split2(values)
        out_ref[:, 0:stop] += applied(product_t, sides_ref[:, columns], high, low)
        if start:
            out_ref[:, columns] += applied(product, sides_ref[:, 0:start], high[0:start], low[0:start])


def call(body, name, shapes, cost):
    return pl.pallas_call(
        body,
        out_shape=shapes,
        compiler_params=pltpu.CompilerParams(vmem_limit_bytes=VMEM_LIMIT),
        cost_estimate=pl.CostEstimate(flops=cost, bytes_accessed=600000, transcendentals=0),
        name=name,
    )


def shape(rows, columns, dtype=f32):
    return jax.ShapeDtypeStruct((rows, columns), dtype)


def prepare(packed):
    rows, sites = packed.shape
    shapes = (shape(sites, 64, bf16), shape(2 * (rows - 8), sites, bf16))
    return call(prepare_body, "prepare", shapes, 10**7)(packed)


def pairs(left, sides, fars):
    count, sites = len(fars), fars[0].shape[1]
    body = functools.partial(pairs_body, count)
    shapes = (shape(16, sites), shape(16 * count, sites))
    return call(body, "pairs%d" % count, shapes, 6 * count * 10**9)(left, sides, *fars)


def own_block(left, sides, packed):
    return call(self_body, "own", shape(16, packed.shape[1]), 4 * 10**9)(left, sides, packed)


def shifted(value, steps):
    count = lax.axis_size(AXES)
    pairs = [(source, (source + steps) % count) for source in range(count)]
    return lax.ppermute(value, AXES, pairs)


def total(values):
    for axis in ("lo", "hi"):
        count = lax.axis_size(axis)
        copies = jnp.broadcast_to(values[None], (count,) + values.shape)
        values = jnp.sum(lax.all_to_all(copies, axis, 0, 0, tiled=True), axis=0)
    return values


def local(coords, inv_scale, noise_var, solution, residual, direction):
    rhs = direction.shape[0]
    scaled = coords * (inv_scale * COORD_SCALE)[:, None]
    packed = jnp.concatenate([scaled, direction * SCALE], axis=0)
    left, sides = prepare(packed)
    gp_image = noise_var[None, :] * direction
    offsets = (-2, 3, 1)
    fars = [shifted(packed, offset) for offset in offsets]
    returns = []
    for offset, far in zip(offsets, fars):
        near, back = pairs(left, sides, [far])
        gp_image = gp_image + near
        returns.append(shifted(back, -offset))
    gp_image = gp_image + (2.0 * ROUNDS) * own_block(left, sides, packed)
    for back in returns:
        gp_image = gp_image + back
    sums = [
        jnp.sum(residual * residual, axis=1),
        jnp.sum(direction * gp_image, axis=1),
        jnp.sum(residual * gp_image, axis=1),
        jnp.sum(gp_image * gp_image, axis=1),
    ]
    sums = total(jnp.concatenate(sums)).reshape(4, rhs)
    old_norm, curvature, mixed, image_norm = sums[0], sums[1], sums[2], sums[3]
    step_size = old_norm / curvature
    new_norm = jnp.maximum(old_norm + step_size * (step_size * image_norm - 2.0 * mixed), 0.0)
    new_solution = solution + step_size[:, None] * direction
    new_residual = residual - step_size[:, None] * gp_image
    new_direction = new_residual + (new_norm / old_norm)[:, None] * direction
    return (new_solution, new_residual, new_direction)


def solution(mesh):
    devices = mesh.devices.reshape(-1)
    low = 32
    split = Mesh(devices.reshape(devices.size // low, low), AXES)
    columns = P(None, AXES)
    return jax.shard_map(
        local,
        mesh=split,
        in_specs=(columns, P(), P(AXES), columns, columns, columns),
        out_specs=(columns, columns, columns),
        check_vma=False,
    )
```

```python
import functools
import math

import jax
import jax.numpy as jnp
from jax import lax
from jax.experimental import pallas as pl
from jax.experimental.pallas import tpu as pltpu
from jax.sharding import Mesh, PartitionSpec as P

ROUNDS = 3
TILE = 256
AXES = ("hi", "lo")
VMEM_LIMIT = 40 * 1024 * 1024

LN2 = math.log(2.0)
COORD_SCALE = math.sqrt(5.0) / LN2
SCALE = LN2 * LN2 / 3.0
LINEAR = 3.0 / LN2
CONSTANT = 1.0 / SCALE
TINY = 1e-30

bf16 = jnp.bfloat16
f32 = jnp.float32


def split2(value):
    high = value.astype(bf16)
    return high, (value - high.astype(f32)).astype(bf16)


def split3(value):
    high = value.astype(bf16).astype(f32)
    rest = value - high
    middle = rest.astype(bf16).astype(f32)
    low = (rest - middle).astype(bf16).astype(f32)
    return high, middle, low


def stacked(value):
    return jnp.concatenate(split2(value), axis=0)


def features(scaled, left):
    high, middle, low = split3(-2.0 * scaled if left else scaled)
    norm = split3(jnp.sum(scaled * scaled, axis=0, keepdims=True))
    row = lax.broadcasted_iota(jnp.int32, scaled.shape, 0)
    first = 0 if left else 3
    extra = jnp.where((row >= 3 - first) & (row < 6 - first), 1.0, 0.0)
    for place, part in enumerate(norm):
        extra = jnp.where(row == first + place, part, extra)
    zero = jnp.zeros_like(extra)
    if left:
        pieces = (high, high, middle, high, middle, low, extra, zero)
    else:
        pieces = (high, middle, high, low, middle, high, extra, zero)
    return jnp.concatenate(pieces, axis=0)


def covariance(squared):
    squared = jnp.maximum(squared, TINY)
    dist = squared * lax.rsqrt(squared)
    return ((dist + LINEAR) * dist + CONSTANT) * jnp.exp2(-dist)


def product(left, right):
    return jnp.dot(left, right, preferred_element_type=f32)


def product_t(left, right):
    return lax.dot_general(left, right, (((1,), (1,)), ((), ())), preferred_element_type=f32)


def applied(dot, sides, high, low):
    rows = sides.shape[0] // 2
    both = dot(sides, high)
    return both[:rows] + both[rows:] + dot(sides[:rows], low)


def prepare_body(packed_ref, left_ref, sides_ref):
    left_ref[...] = features(packed_ref[0:8, :], True).T.astype(bf16)
    sides_ref[...] = stacked(packed_ref[8:24, :])


def block_products(left, sides, far_ref, base_ref, near_ref, back_ref):
    sites = far_ref.shape[1]
    right = features(far_ref[0:8, :], False).astype(bf16)
    far_sides = stacked(far_ref[8:24, :])
    near = None
    for start in range(0, sites, TILE):
        columns = slice(start, start + TILE)
        values = covariance(product(left, right[:, columns]))
        high, low = split2(values)
        part = applied(product_t, far_sides[:, columns], high, low)
        near = part if near is None else near + part
        back = applied(product, sides, high, low)
        back_ref[:, columns] = back if base_ref is None else back + base_ref[:, columns]
    near_ref[...] = near


def own_pair_body(left_ref, sides_ref, far_ref, *refs):
    base_ref = refs[0] if len(refs) == 3 else None
    block_products(left_ref[...], sides_ref[...], far_ref, base_ref, refs[-2], refs[-1])


def far_pair_body(one_ref, other_ref, base_ref, near_ref, back_ref):
    left = features(one_ref[0:8, :], True).T.astype(bf16)
    block_products(left, stacked(one_ref[8:24, :]), other_ref, base_ref, near_ref, back_ref)


def self_body(left_ref, sides_ref, own_ref, out_ref):
    sites = own_ref.shape[1]
    right = features(own_ref[0:8, :], False).astype(bf16)
    out_ref[...] = jnp.zeros_like(out_ref)
    for start in range(0, sites, TILE):
        stop = start + TILE
        columns = slice(start, stop)
        values = covariance(product(left_ref[0:stop, :], right[:, columns]))
        high, low = split2(values)
        out_ref[:, 0:stop] += applied(product_t, sides_ref[:, columns], high, low)
        if start:
            out_ref[:, columns] += applied(product, sides_ref[:, 0:start], high[0:start], low[0:start])


def call(body, name, shapes, cost):
    return pl.pallas_call(
        body,
        out_shape=shapes,
        compiler_params=pltpu.CompilerParams(vmem_limit_bytes=VMEM_LIMIT),
        cost_estimate=pl.CostEstimate(flops=cost, bytes_accessed=600000, transcendentals=0),
        name=name,
    )


def shape(rows, columns, dtype=f32):
    return jax.ShapeDtypeStruct((rows, columns), dtype)


def prepare(packed):
    rows, sites = packed.shape
    shapes = (shape(sites, 64, bf16), shape(2 * (rows - 8), sites, bf16))
    return call(prepare_body, "prepare", shapes, 10**7)(packed)


def own_pair(left, sides, far, *base):
    out = shape(16, far.shape[1])
    return call(own_pair_body, "own_pair", (out, out), 6 * 10**9)(left, sides, far, *base)


def far_pair(one, other, base):
    out = shape(16, one.shape[1])
    return call(far_pair_body, "far_pair", (out, out), 6 * 10**9)(one, other, base)


def own_block(left, sides, packed):
    return call(self_body, "own", shape(16, packed.shape[1]), 4 * 10**9)(left, sides, packed)


def shifted(value, steps):
    count = lax.axis_size(AXES)
    pairs = [(source, (source + steps) % count) for source in range(count)]
    return lax.ppermute(value, AXES, pairs)


def total(values):
    for axis in ("lo", "hi"):
        count = lax.axis_size(axis)
        copies = jnp.broadcast_to(values[None], (count,) + values.shape)
        values = jnp.sum(lax.all_to_all(copies, axis, 0, 0, tiled=True), axis=0)
    return values


def local(coords, inv_scale, noise_var, solution, residual, direction):
    rhs = direction.shape[0]
    scaled = (coords * COORD_SCALE) * inv_scale[:, None]
    packed = jnp.concatenate([scaled, direction * SCALE], axis=0)
    right = shifted(packed, -1)
    left2 = shifted(packed, 2)
    left, sides = prepare(packed)
    near_right, to_right = own_pair(left, sides, right)
    to_left2, to_right = far_pair(left2, right, to_right)
    from_left = shifted(to_right, 1)
    near_left2, to_left2 = own_pair(left, sides, left2, to_left2)
    from_right2 = shifted(to_left2, -2)
    own = own_block(left, sides, packed)
    gp_image = noise_var[None, :] * direction + near_right + near_left2 + (2.0 * ROUNDS) * own + from_left + from_right2
    sums = [
        jnp.sum(residual * residual, axis=1),
        jnp.sum(direction * gp_image, axis=1),
        jnp.sum(residual * gp_image, axis=1),
        jnp.sum(gp_image * gp_image, axis=1),
    ]
    sums = total(jnp.concatenate(sums)).reshape(4, rhs)
    old_norm, curvature, mixed, image_norm = sums[0], sums[1], sums[2], sums[3]
    step_size = old_norm / curvature
    new_norm = jnp.maximum(old_norm + step_size * (step_size * image_norm - 2.0 * mixed), 0.0)
    new_solution = solution + step_size[:, None] * direction
    new_residual = residual - step_size[:, None] * gp_image
    new_direction = new_residual + (new_norm / old_norm)[:, None] * direction
    return (new_solution, new_residual, new_direction)


def solution(mesh):
    devices = mesh.devices.reshape(-1)
    low = 32
    split = Mesh(devices.reshape(devices.size // low, low), AXES)
    columns = P(None, AXES)
    return jax.shard_map(
        local,
        mesh=split,
        in_specs=(columns, P(), P(AXES), columns, columns, columns),
        out_specs=(columns, columns, columns),
        check_vma=False,
    )
```

```python
import functools
import math

import jax
import jax.numpy as jnp
from jax import lax
from jax.experimental import pallas as pl
from jax.experimental.pallas import tpu as pltpu
from jax.sharding import Mesh, PartitionSpec as P

ROUNDS = 3
TILE = 256
AXES = ("hi", "lo")
VMEM_LIMIT = 40 * 1024 * 1024

LN2 = math.log(2.0)
COORD_SCALE = math.sqrt(5.0) / LN2
SCALE = LN2 * LN2 / 3.0
LINEAR = 3.0 / LN2
CONSTANT = 1.0 / SCALE
TINY = 1e-30

bf16 = jnp.bfloat16
f32 = jnp.float32


def split2(value):
    high = value.astype(bf16)
    return high, (value - high.astype(f32)).astype(bf16)


def split3(value):
    high = value.astype(bf16).astype(f32)
    rest = value - high
    middle = rest.astype(bf16).astype(f32)
    low = (rest - middle).astype(bf16).astype(f32)
    return high, middle, low


def stacked(value):
    return jnp.concatenate(split2(value), axis=0)


def features(scaled, left):
    high, middle, low = split3(-2.0 * scaled if left else scaled)
    norm = split3(jnp.sum(scaled * scaled, axis=0, keepdims=True))
    row = lax.broadcasted_iota(jnp.int32, scaled.shape, 0)
    first = 0 if left else 3
    extra = jnp.where((row >= 3 - first) & (row < 6 - first), 1.0, 0.0)
    for place, part in enumerate(norm):
        extra = jnp.where(row == first + place, part, extra)
    zero = jnp.zeros_like(extra)
    if left:
        pieces = (high, high, middle, high, middle, low, extra, zero)
    else:
        pieces = (high, middle, high, low, middle, high, extra, zero)
    return jnp.concatenate(pieces, axis=0)


def covariance(squared):
    squared = jnp.maximum(squared, TINY)
    dist = squared * lax.rsqrt(squared)
    return ((dist + LINEAR) * dist + CONSTANT) * jnp.exp2(-dist)


def product(left, right):
    return jnp.dot(left, right, preferred_element_type=f32)


def product_t(left, right):
    return lax.dot_general(left, right, (((1,), (1,)), ((), ())), preferred_element_type=f32)


def applied(dot, sides, high, low):
    rows = sides.shape[0] // 2
    both = dot(sides, high)
    return both[:rows] + both[rows:] + dot(sides[:rows], low)


def left_side(packed_ref, inv_ref):
    scaled = packed_ref[0:8, :] * (inv_ref[...] * COORD_SCALE)
    return features(scaled, True).T.astype(bf16), stacked(packed_ref[8:24, :] * SCALE)


def right_side(packed_ref, inv_ref):
    scaled = packed_ref[0:8, :] * (inv_ref[...] * COORD_SCALE)
    return features(scaled, False).astype(bf16), stacked(packed_ref[8:24, :] * SCALE)


def prepare_body(packed_ref, inv_ref, left_ref, sides_ref):
    left_ref[...], sides_ref[...] = left_side(packed_ref, inv_ref)


def block_products(left, sides, far_ref, inv_ref, base_ref, near_ref, back_ref):
    sites = far_ref.shape[1]
    right, far_sides = right_side(far_ref, inv_ref)
    near = None
    for start in range(0, sites, TILE):
        columns = slice(start, start + TILE)
        values = covariance(product(left, right[:, columns]))
        high, low = split2(values)
        part = applied(product_t, far_sides[:, columns], high, low)
        near = part if near is None else near + part
        back = applied(product, sides, high, low)
        back_ref[:, columns] = back if base_ref is None else back + base_ref[:, columns]
    near_ref[...] = near


def own_pair_body(left_ref, sides_ref, far_ref, inv_ref, *refs):
    base_ref = refs[0] if len(refs) == 3 else None
    block_products(left_ref[...], sides_ref[...], far_ref, inv_ref, base_ref, refs[-2], refs[-1])


def far_pair_body(one_ref, other_ref, inv_ref, base_ref, near_ref, back_ref):
    left, sides = left_side(one_ref, inv_ref)
    block_products(left, sides, other_ref, inv_ref, base_ref, near_ref, back_ref)


def self_body(left_ref, sides_ref, own_ref, inv_ref, base_ref, out_ref):
    sites = own_ref.shape[1]
    right, _ = right_side(own_ref, inv_ref)
    out_ref[...] = jnp.zeros_like(out_ref)
    for start in range(0, sites, TILE):
        stop = start + TILE
        columns = slice(start, stop)
        values = covariance(product(left_ref[0:stop, :], right[:, columns]))
        high, low = split2(values)
        out_ref[:, 0:stop] += applied(product_t, sides_ref[:, columns], high, low)
        if start:
            out_ref[:, columns] += applied(product, sides_ref[:, 0:start], high[0:start], low[0:start])
    out_ref[...] = (2.0 * ROUNDS) * out_ref[...] + base_ref[...]


def call(body, name, shapes, cost):
    return pl.pallas_call(
        body,
        out_shape=shapes,
        compiler_params=pltpu.CompilerParams(vmem_limit_bytes=VMEM_LIMIT),
        cost_estimate=pl.CostEstimate(flops=cost, bytes_accessed=600000, transcendentals=0),
        name=name,
    )


def shape(rows, columns, dtype=f32):
    return jax.ShapeDtypeStruct((rows, columns), dtype)


def prepare(packed, inv):
    rows, sites = packed.shape
    shapes = (shape(sites, 64, bf16), shape(2 * (rows - 8), sites, bf16))
    return call(prepare_body, "prepare", shapes, 10**7)(packed, inv)


def own_pair(left, sides, far, inv, *base):
    out = shape(16, far.shape[1])
    return call(own_pair_body, "own_pair", (out, out), 6 * 10**9)(left, sides, far, inv, *base)


def far_pair(one, other, inv, base):
    out = shape(16, one.shape[1])
    return call(far_pair_body, "far_pair", (out, out), 6 * 10**9)(one, other, inv, base)


def own_block(left, sides, packed, inv, base):
    return call(self_body, "own", shape(16, packed.shape[1]), 4 * 10**9)(left, sides, packed, inv, base)


def shifted(value, steps):
    count = lax.axis_size(AXES)
    pairs = [(source, (source + steps) % count) for source in range(count)]
    return lax.ppermute(value, AXES, pairs)


def total(values):
    for axis in ("lo", "hi"):
        count = lax.axis_size(axis)
        copies = jnp.broadcast_to(values[None], (count,) + values.shape)
        values = jnp.sum(lax.all_to_all(copies, axis, 0, 0, tiled=True), axis=0)
    return values


def local(coords, inv_scale, noise_var, solution, residual, direction):
    rhs = direction.shape[0]
    packed = jnp.concatenate([coords, direction], axis=0)
    inv = inv_scale[:, None]
    right = shifted(packed, -1)
    left2 = shifted(packed, 2)
    left, sides = prepare(packed, inv)
    near_right, to_right = own_pair(left, sides, right, inv)
    to_left2, to_right = far_pair(left2, right, inv, to_right)
    from_left = shifted(to_right, 1)
    near_left2, to_left2 = own_pair(left, sides, left2, inv, to_left2)
    from_right2 = shifted(to_left2, -2)
    own = own_block(left, sides, packed, inv, from_left)
    gp_image = noise_var[None, :] * direction + near_right + near_left2 + own + from_right2
    sums = [
        jnp.sum(residual * residual, axis=1),
        jnp.sum(direction * gp_image, axis=1),
        jnp.sum(residual * gp_image, axis=1),
        jnp.sum(gp_image * gp_image, axis=1),
    ]
    sums = total(jnp.concatenate(sums)).reshape(4, rhs)
    old_norm, curvature, mixed, image_norm = sums[0], sums[1], sums[2], sums[3]
    step_size = old_norm / curvature
    new_norm = jnp.maximum(old_norm + step_size * (step_size * image_norm - 2.0 * mixed), 0.0)
    new_solution = solution + step_size[:, None] * direction
    new_residual = residual - step_size[:, None] * gp_image
    new_direction = new_residual + (new_norm / old_norm)[:, None] * direction
    return (new_solution, new_residual, new_direction)


def solution(mesh):
    devices = mesh.devices.reshape(-1)
    low = 32
    split = Mesh(devices.reshape(devices.size // low, low), AXES)
    columns = P(None, AXES)
    return jax.shard_map(
        local,
        mesh=split,
        in_specs=(columns, P(), P(AXES), columns, columns, columns),
        out_specs=(columns, columns, columns),
        check_vma=False,
    )
```

```python
import functools
import math

import jax
import jax.numpy as jnp
from jax import lax
from jax.experimental import pallas as pl
from jax.experimental.pallas import tpu as pltpu
from jax.sharding import Mesh, PartitionSpec as P

ROUNDS = 3
TILE = 256
AXES = ("hi", "lo")
VMEM_LIMIT = 40 * 1024 * 1024

LN2 = math.log(2.0)
COORD_SCALE = math.sqrt(5.0) / LN2
SCALE = LN2 * LN2 / 3.0
LINEAR = 3.0 / LN2
CONSTANT = 1.0 / SCALE
TINY = 1e-30

bf16 = jnp.bfloat16
f32 = jnp.float32


def split2(value):
    high = value.astype(bf16)
    return high, (value - high.astype(f32)).astype(bf16)


def split3(value):
    high = value.astype(bf16).astype(f32)
    rest = value - high
    middle = rest.astype(bf16).astype(f32)
    low = (rest - middle).astype(bf16).astype(f32)
    return high, middle, low


def stacked(value):
    return jnp.concatenate(split2(value), axis=0)


def features(scaled, left):
    high, middle, low = split3(-2.0 * scaled if left else scaled)
    norm = split3(jnp.sum(scaled * scaled, axis=0, keepdims=True))
    row = lax.broadcasted_iota(jnp.int32, scaled.shape, 0)
    first = 0 if left else 3
    extra = jnp.where((row >= 3 - first) & (row < 6 - first), 1.0, 0.0)
    for place, part in enumerate(norm):
        extra = jnp.where(row == first + place, part, extra)
    zero = jnp.zeros_like(extra)
    if left:
        pieces = (high, high, middle, high, middle, low, extra, zero)
    else:
        pieces = (high, middle, high, low, middle, high, extra, zero)
    return jnp.concatenate(pieces, axis=0)


def covariance(squared):
    squared = jnp.maximum(squared, TINY)
    dist = squared * lax.rsqrt(squared)
    return ((dist + LINEAR) * dist + CONSTANT) * jnp.exp2(-dist)


def product(left, right):
    return jnp.dot(left, right, preferred_element_type=f32)


def product_t(left, right):
    return lax.dot_general(left, right, (((1,), (1,)), ((), ())), preferred_element_type=f32)


def applied(dot, sides, high, low):
    rows = sides.shape[0] // 2
    both = dot(sides, high)
    return both[:rows] + both[rows:] + dot(sides[:rows], low)


def left_side(packed_ref, inv_ref):
    scaled = packed_ref[0:8, :] * (inv_ref[...] * COORD_SCALE)
    return features(scaled, True).T.astype(bf16), stacked(packed_ref[8:24, :] * SCALE)


def right_side(packed_ref, inv_ref):
    scaled = packed_ref[0:8, :] * (inv_ref[...] * COORD_SCALE)
    return features(scaled, False).astype(bf16), stacked(packed_ref[8:24, :] * SCALE)


def prepare_body(packed_ref, inv_ref, left_ref, sides_ref):
    left_ref[...], sides_ref[...] = left_side(packed_ref, inv_ref)


def block_products(left, sides, far_ref, inv_ref, base_ref, near_ref, back_ref):
    sites = far_ref.shape[1]
    right, far_sides = right_side(far_ref, inv_ref)
    near = None
    for start in range(0, sites, TILE):
        columns = slice(start, start + TILE)
        values = covariance(product(left, right[:, columns]))
        high, low = split2(values)
        part = applied(product_t, far_sides[:, columns], high, low)
        near = part if near is None else near + part
        back = applied(product, sides, high, low)
        back_ref[:, columns] = back if base_ref is None else back + base_ref[:, columns]
    near_ref[...] = near


def own_pair_body(left_ref, sides_ref, far_ref, inv_ref, *refs):
    base_ref = refs[0] if len(refs) == 3 else None
    block_products(left_ref[...], sides_ref[...], far_ref, inv_ref, base_ref, refs[-2], refs[-1])


def far_pair_body(one_ref, other_ref, inv_ref, base_ref, near_ref, back_ref):
    left, sides = left_side(one_ref, inv_ref)
    block_products(left, sides, other_ref, inv_ref, base_ref, near_ref, back_ref)


def self_body(left_ref, sides_ref, own_ref, inv_ref, base_ref, out_ref):
    sites = own_ref.shape[1]
    right, _ = right_side(own_ref, inv_ref)
    out_ref[...] = jnp.zeros_like(out_ref)
    for start in range(0, sites, TILE):
        stop = start + TILE
        columns = slice(start, stop)
        values = covariance(product(left_ref[0:stop, :], right[:, columns]))
        high, low = split2(values)
        out_ref[:, 0:stop] += applied(product_t, sides_ref[:, columns], high, low)
        if start:
            out_ref[:, columns] += applied(product, sides_ref[:, 0:start], high[0:start], low[0:start])
    out_ref[...] = (2.0 * ROUNDS) * out_ref[...] + base_ref[...]


def call(body, name, shapes, cost):
    return pl.pallas_call(
        body,
        out_shape=shapes,
        compiler_params=pltpu.CompilerParams(vmem_limit_bytes=VMEM_LIMIT),
        cost_estimate=pl.CostEstimate(flops=cost, bytes_accessed=600000, transcendentals=0),
        name=name,
    )


def shape(rows, columns, dtype=f32):
    return jax.ShapeDtypeStruct((rows, columns), dtype)


def prepare(packed, inv):
    rows, sites = packed.shape
    shapes = (shape(sites, 64, bf16), shape(2 * (rows - 8), sites, bf16))
    return call(prepare_body, "prepare", shapes, 10**7)(packed, inv)


def own_pair(left, sides, far, inv, *base):
    out = shape(16, far.shape[1])
    return call(own_pair_body, "own_pair", (out, out), 6 * 10**9)(left, sides, far, inv, *base)


def far_pair(one, other, inv, base):
    out = shape(16, one.shape[1])
    return call(far_pair_body, "far_pair", (out, out), 6 * 10**9)(one, other, inv, base)


def own_block(left, sides, packed, inv, base):
    return call(self_body, "own", shape(16, packed.shape[1]), 4 * 10**9)(left, sides, packed, inv, base)


def shifted(value, steps):
    count = lax.axis_size(AXES)
    pairs = [(source, (source + steps) % count) for source in range(count)]
    return lax.ppermute(value, AXES, pairs)


def total(values):
    for axis in ("lo", "hi"):
        count = lax.axis_size(axis)
        copies = jnp.broadcast_to(values[None], (count,) + values.shape)
        values = jnp.sum(lax.all_to_all(copies, axis, 0, 0, tiled=True), axis=0)
    return values


def local(coords, inv_scale, noise_var, solution, residual, direction):
    rhs = direction.shape[0]
    packed = jnp.concatenate([coords, direction], axis=0)
    inv = inv_scale[:, None]
    left2 = shifted(packed, 2)
    right = shifted(packed, -1)
    left, sides = prepare(packed, inv)
    near_left2, to_left2 = own_pair(left, sides, left2, inv)
    to_right, to_left2 = far_pair(right, left2, inv, to_left2)
    from_right2 = shifted(to_left2, -2)
    near_right, to_right = own_pair(left, sides, right, inv, to_right)
    from_left = shifted(to_right, 1)
    own = own_block(left, sides, packed, inv, from_right2)
    gp_image = noise_var[None, :] * direction + near_right + near_left2 + own + from_left
    sums = [
        jnp.sum(residual * residual, axis=1),
        jnp.sum(direction * gp_image, axis=1),
        jnp.sum(residual * gp_image, axis=1),
        jnp.sum(gp_image * gp_image, axis=1),
    ]
    sums = total(jnp.concatenate(sums)).reshape(4, rhs)
    old_norm, curvature, mixed, image_norm = sums[0], sums[1], sums[2], sums[3]
    step_size = old_norm / curvature
    new_norm = jnp.maximum(old_norm + step_size * (step_size * image_norm - 2.0 * mixed), 0.0)
    new_solution = solution + step_size[:, None] * direction
    new_residual = residual - step_size[:, None] * gp_image
    new_direction = new_residual + (new_norm / old_norm)[:, None] * direction
    return (new_solution, new_residual, new_direction)


def solution(mesh):
    devices = mesh.devices.reshape(-1)
    low = 32
    split = Mesh(devices.reshape(devices.size // low, low), AXES)
    columns = P(None, AXES)
    return jax.shard_map(
        local,
        mesh=split,
        in_specs=(columns, P(), P(AXES), columns, columns, columns),
        out_specs=(columns, columns, columns),
        check_vma=False,
    )
```

```python
import functools
import math

import jax
import jax.numpy as jnp
from jax import lax
from jax.experimental import pallas as pl
from jax.experimental.pallas import tpu as pltpu
from jax.sharding import Mesh, PartitionSpec as P

ROUNDS = 3
TILE = 256
AXES = ("hi", "lo")
VMEM_LIMIT = 40 * 1024 * 1024

LN2 = math.log(2.0)
COORD_SCALE = math.sqrt(5.0) / LN2
SCALE = LN2 * LN2 / 3.0
LINEAR = 3.0 / LN2
CONSTANT = 1.0 / SCALE
TINY = 1e-30

bf16 = jnp.bfloat16
f32 = jnp.float32


def split2(value):
    high = value.astype(bf16)
    return high, (value - high.astype(f32)).astype(bf16)


def split3(value):
    high = value.astype(bf16).astype(f32)
    rest = value - high
    middle = rest.astype(bf16).astype(f32)
    low = (rest - middle).astype(bf16).astype(f32)
    return high, middle, low


def stacked(value):
    return jnp.concatenate(split2(value), axis=0)


def features(scaled, left):
    high, middle, low = split3(-2.0 * scaled if left else scaled)
    norm = split3(jnp.sum(scaled * scaled, axis=0, keepdims=True))
    row = lax.broadcasted_iota(jnp.int32, scaled.shape, 0)
    first = 0 if left else 3
    extra = jnp.where((row >= 3 - first) & (row < 6 - first), 1.0, 0.0)
    for place, part in enumerate(norm):
        extra = jnp.where(row == first + place, part, extra)
    zero = jnp.zeros_like(extra)
    if left:
        pieces = (high, high, middle, high, middle, low, extra, zero)
    else:
        pieces = (high, middle, high, low, middle, high, extra, zero)
    return jnp.concatenate(pieces, axis=0)


def covariance(squared):
    squared = jnp.maximum(squared, TINY)
    less = -squared * lax.rsqrt(squared)
    return ((squared + CONSTANT) - LINEAR * less) * jnp.exp2(less)


def product(left, right):
    return jnp.dot(left, right, preferred_element_type=f32)


def product_t(left, right):
    return lax.dot_general(left, right, (((1,), (1,)), ((), ())), preferred_element_type=f32)


def applied(dot, sides, high, low):
    rows = sides.shape[0] // 2
    both = dot(sides, high)
    return both[:rows] + both[rows:] + dot(sides[:rows], low)


def left_side(packed_ref, inv_ref):
    scaled = packed_ref[0:8, :] * (inv_ref[...] * COORD_SCALE)
    return features(scaled, True).T.astype(bf16), stacked(packed_ref[8:24, :] * SCALE)


def right_side(packed_ref, inv_ref):
    scaled = packed_ref[0:8, :] * (inv_ref[...] * COORD_SCALE)
    return features(scaled, False).astype(bf16), stacked(packed_ref[8:24, :] * SCALE)


def prepare_body(packed_ref, inv_ref, left_ref, sides_ref):
    left_ref[...], sides_ref[...] = left_side(packed_ref, inv_ref)


def block_products(left, sides, far_ref, inv_ref, base_ref, near_ref, back_ref):
    sites = far_ref.shape[1]
    right, far_sides = right_side(far_ref, inv_ref)
    near = None
    for start in range(0, sites, TILE):
        columns = slice(start, start + TILE)
        values = covariance(product(left, right[:, columns]))
        high, low = split2(values)
        part = applied(product_t, far_sides[:, columns], high, low)
        near = part if near is None else near + part
        back = applied(product, sides, high, low)
        back_ref[:, columns] = back if base_ref is None else back + base_ref[:, columns]
    near_ref[...] = near


def own_pair_body(left_ref, sides_ref, far_ref, inv_ref, *refs):
    base_ref = refs[0] if len(refs) == 3 else None
    block_products(left_ref[...], sides_ref[...], far_ref, inv_ref, base_ref, refs[-2], refs[-1])


def far_pair_body(one_ref, other_ref, inv_ref, base_ref, near_ref, back_ref):
    left, sides = left_side(one_ref, inv_ref)
    block_products(left, sides, other_ref, inv_ref, base_ref, near_ref, back_ref)


def self_body(left_ref, sides_ref, own_ref, inv_ref, base_ref, out_ref):
    sites = own_ref.shape[1]
    right, _ = right_side(own_ref, inv_ref)
    out_ref[...] = jnp.zeros_like(out_ref)
    for start in range(0, sites, TILE):
        stop = start + TILE
        columns = slice(start, stop)
        values = covariance(product(left_ref[0:stop, :], right[:, columns]))
        high, low = split2(values)
        out_ref[:, 0:stop] += applied(product_t, sides_ref[:, columns], high, low)
        if start:
            out_ref[:, columns] += applied(product, sides_ref[:, 0:start], high[0:start], low[0:start])
    out_ref[...] = (2.0 * ROUNDS) * out_ref[...] + base_ref[...]


def call(body, name, shapes, cost):
    return pl.pallas_call(
        body,
        out_shape=shapes,
        compiler_params=pltpu.CompilerParams(vmem_limit_bytes=VMEM_LIMIT),
        cost_estimate=pl.CostEstimate(flops=cost, bytes_accessed=600000, transcendentals=0),
        name=name,
    )


def shape(rows, columns, dtype=f32):
    return jax.ShapeDtypeStruct((rows, columns), dtype)


def prepare(packed, inv):
    rows, sites = packed.shape
    shapes = (shape(sites, 64, bf16), shape(2 * (rows - 8), sites, bf16))
    return call(prepare_body, "prepare", shapes, 10**7)(packed, inv)


def own_pair(left, sides, far, inv, *base):
    out = shape(16, far.shape[1])
    return call(own_pair_body, "own_pair", (out, out), 6 * 10**9)(left, sides, far, inv, *base)


def far_pair(one, other, inv, base):
    out = shape(16, one.shape[1])
    return call(far_pair_body, "far_pair", (out, out), 6 * 10**9)(one, other, inv, base)


def own_block(left, sides, packed, inv, base):
    return call(self_body, "own", shape(16, packed.shape[1]), 4 * 10**9)(left, sides, packed, inv, base)


def shifted(value, steps):
    count = lax.axis_size(AXES)
    pairs = [(source, (source + steps) % count) for source in range(count)]
    return lax.ppermute(value, AXES, pairs)


def total(values):
    for axis in ("lo", "hi"):
        count = lax.axis_size(axis)
        copies = jnp.broadcast_to(values[None], (count,) + values.shape)
        values = jnp.sum(lax.all_to_all(copies, axis, 0, 0, tiled=True), axis=0)
    return values


def local(coords, inv_scale, noise_var, solution, residual, direction):
    rhs = direction.shape[0]
    packed = jnp.concatenate([coords, direction], axis=0)
    inv = inv_scale[:, None]
    left2 = shifted(packed, 2)
    right = shifted(packed, -1)
    left, sides = prepare(packed, inv)
    near_left2, to_left2 = own_pair(left, sides, left2, inv)
    to_right, to_left2 = far_pair(right, left2, inv, to_left2)
    from_right2 = shifted(to_left2, -2)
    near_right, to_right = own_pair(left, sides, right, inv, to_right)
    from_left = shifted(to_right, 1)
    own = own_block(left, sides, packed, inv, from_right2)
    gp_image = noise_var[None, :] * direction + near_right + near_left2 + own + from_left
    sums = [
        jnp.sum(residual * residual, axis=1),
        jnp.sum(direction * gp_image, axis=1),
        jnp.sum(residual * gp_image, axis=1),
        jnp.sum(gp_image * gp_image, axis=1),
    ]
    sums = total(jnp.concatenate(sums)).reshape(4, rhs)
    old_norm, curvature, mixed, image_norm = sums[0], sums[1], sums[2], sums[3]
    step_size = old_norm / curvature
    new_norm = jnp.maximum(old_norm + step_size * (step_size * image_norm - 2.0 * mixed), 0.0)
    new_solution = solution + step_size[:, None] * direction
    new_residual = residual - step_size[:, None] * gp_image
    new_direction = new_residual + (new_norm / old_norm)[:, None] * direction
    return (new_solution, new_residual, new_direction)


def solution(mesh):
    devices = mesh.devices.reshape(-1)
    low = 32
    split = Mesh(devices.reshape(devices.size // low, low), AXES)
    columns = P(None, AXES)
    return jax.shard_map(
        local,
        mesh=split,
        in_specs=(columns, P(), P(AXES), columns, columns, columns),
        out_specs=(columns, columns, columns),
        check_vma=False,
    )
```

```python
import functools
import math

import jax
import jax.numpy as jnp
from jax import lax
from jax.experimental import pallas as pl
from jax.experimental.pallas import tpu as pltpu
from jax.sharding import Mesh, PartitionSpec as P

ROUNDS = 3
TILE = 256
AXES = ("hi", "lo")
VMEM_LIMIT = 40 * 1024 * 1024

LN2 = math.log(2.0)
COORD_SCALE = math.sqrt(5.0) / LN2
SCALE = LN2 * LN2 / 3.0
LINEAR = 3.0 / LN2
CONSTANT = 1.0 / SCALE
TINY = 1e-30

bf16 = jnp.bfloat16
f32 = jnp.float32


def split2(value):
    high = value.astype(bf16)
    return high, (value - high.astype(f32)).astype(bf16)


def split3(value):
    high = value.astype(bf16).astype(f32)
    rest = value - high
    middle = rest.astype(bf16).astype(f32)
    low = (rest - middle).astype(bf16).astype(f32)
    return high, middle, low


def stacked(value):
    return jnp.concatenate(split2(value), axis=0)


def features(scaled, left):
    high, middle, low = split3(-2.0 * scaled if left else scaled)
    norm = split3(jnp.sum(scaled * scaled, axis=0, keepdims=True))
    row = lax.broadcasted_iota(jnp.int32, scaled.shape, 0)
    first = 0 if left else 3
    extra = jnp.where((row >= 3 - first) & (row < 6 - first), 1.0, 0.0)
    for place, part in enumerate(norm):
        extra = jnp.where(row == first + place, part, extra)
    zero = jnp.zeros_like(extra)
    if left:
        pieces = (high, high, middle, high, middle, low, extra, zero)
    else:
        pieces = (high, middle, high, low, middle, high, extra, zero)
    return jnp.concatenate(pieces, axis=0)


def covariance(squared):
    squared = jnp.maximum(squared, TINY)
    less = -squared * lax.rsqrt(squared)
    return ((squared + CONSTANT) - LINEAR * less) * jnp.exp2(less)


def product(left, right):
    return jnp.dot(left, right, preferred_element_type=f32)


def product_t(left, right):
    return lax.dot_general(left, right, (((1,), (1,)), ((), ())), preferred_element_type=f32)


def applied(dot, sides, high, low):
    rows = sides.shape[0] // 2
    both = dot(sides, high)
    return both[:rows] + both[rows:] + dot(sides[:rows], low)


def left_side(packed_ref, inv_ref):
    scaled = packed_ref[0:8, :] * (inv_ref[...] * COORD_SCALE)
    return features(scaled, True).T.astype(bf16), stacked(packed_ref[8:24, :] * SCALE)


def right_side(packed_ref, inv_ref):
    scaled = packed_ref[0:8, :] * (inv_ref[...] * COORD_SCALE)
    return features(scaled, False).astype(bf16), stacked(packed_ref[8:24, :] * SCALE)


def prepare_body(packed_ref, inv_ref, left_ref, sides_ref):
    left_ref[...], sides_ref[...] = left_side(packed_ref, inv_ref)


def block_products(left, sides, far_ref, inv_ref, base_ref, near_ref, back_ref):
    sites = far_ref.shape[1]
    right, far_sides = right_side(far_ref, inv_ref)
    near = None
    for start in range(0, sites, TILE):
        columns = slice(start, start + TILE)
        values = covariance(product(left, right[:, columns]))
        high, low = split2(values)
        part = applied(product_t, far_sides[:, columns], high, low)
        near = part if near is None else near + part
        back = applied(product, sides, high, low)
        back_ref[:, columns] = back if base_ref is None else back + base_ref[:, columns]
    near_ref[...] = near


def own_pair_body(left_ref, sides_ref, far_ref, inv_ref, base_ref, near_ref, back_ref):
    block_products(left_ref[...], sides_ref[...], far_ref, inv_ref, base_ref, near_ref, back_ref)


def first_pair_body(left_ref, sides_ref, far_ref, inv_ref, near_base_ref, near_ref, back_ref):
    block_products(left_ref[...], sides_ref[...], far_ref, inv_ref, None, near_ref, back_ref)
    near_ref[...] += near_base_ref[...]


def far_pair_body(one_ref, other_ref, inv_ref, base_ref, near_ref, back_ref):
    left, sides = left_side(one_ref, inv_ref)
    block_products(left, sides, other_ref, inv_ref, base_ref, near_ref, back_ref)


def self_body(tiles, left_ref, sides_ref, own_ref, inv_ref, *refs):
    out_ref = refs[-1]
    right, _ = right_side(own_ref, inv_ref)
    out_ref[...] = jnp.zeros_like(out_ref)
    for tile in tiles:
        start, stop = tile * TILE, (tile + 1) * TILE
        columns = slice(start, stop)
        values = covariance(product(left_ref[0:stop, :], right[:, columns]))
        high, low = split2(values)
        out_ref[:, 0:stop] += applied(product_t, sides_ref[:, columns], high, low)
        if start:
            out_ref[:, columns] += applied(product, sides_ref[:, 0:start], high[0:start], low[0:start])
    out = (2.0 * ROUNDS) * out_ref[...]
    out_ref[...] = out + refs[0][...] if len(refs) == 2 else out


def call(body, name, shapes, cost):
    return pl.pallas_call(
        body,
        out_shape=shapes,
        compiler_params=pltpu.CompilerParams(vmem_limit_bytes=VMEM_LIMIT),
        cost_estimate=pl.CostEstimate(flops=cost, bytes_accessed=600000, transcendentals=0),
        name=name,
    )


def shape(rows, columns, dtype=f32):
    return jax.ShapeDtypeStruct((rows, columns), dtype)


def prepare(packed, inv):
    rows, sites = packed.shape
    shapes = (shape(sites, 64, bf16), shape(2 * (rows - 8), sites, bf16))
    return call(prepare_body, "prepare", shapes, 10**7)(packed, inv)


def own_pair(left, sides, far, inv, base):
    out = shape(16, far.shape[1])
    return call(own_pair_body, "own_pair", (out, out), 6 * 10**9)(left, sides, far, inv, base)


def first_pair(left, sides, far, inv, near_base):
    out = shape(16, far.shape[1])
    return call(first_pair_body, "first_pair", (out, out), 6 * 10**9)(left, sides, far, inv, near_base)


def far_pair(one, other, inv, base):
    out = shape(16, one.shape[1])
    return call(far_pair_body, "far_pair", (out, out), 6 * 10**9)(one, other, inv, base)


def own_block(tiles, left, sides, packed, inv, *base):
    body = functools.partial(self_body, tiles)
    return call(body, "own", shape(16, packed.shape[1]), 2 * 10**9)(left, sides, packed, inv, *base)


def shifted(value, steps):
    count = lax.axis_size(AXES)
    pairs = [(source, (source + steps) % count) for source in range(count)]
    return lax.ppermute(value, AXES, pairs)


def total(values):
    for axis in ("lo", "hi"):
        count = lax.axis_size(axis)
        copies = jnp.broadcast_to(values[None], (count,) + values.shape)
        values = jnp.sum(lax.all_to_all(copies, axis, 0, 0, tiled=True), axis=0)
    return values


def local(coords, inv_scale, noise_var, solution, residual, direction):
    rhs = direction.shape[0]
    packed = jnp.concatenate([coords, direction], axis=0)
    inv = inv_scale[:, None]
    left2 = shifted(packed, 2)
    right = shifted(packed, -1)
    left, sides = prepare(packed, inv)
    count = packed.shape[1] // TILE
    early = count - count // 3
    own_early = own_block(range(early), left, sides, packed, inv)
    near_left2, to_left2 = first_pair(left, sides, left2, inv, own_early)
    to_right, to_left2 = far_pair(right, left2, inv, to_left2)
    from_right2 = shifted(to_left2, -2)
    near_right, to_right = own_pair(left, sides, right, inv, to_right)
    from_left = shifted(to_right, 1)
    own = own_block(range(early, count), left, sides, packed, inv, from_right2)
    gp_image = noise_var[None, :] * direction + near_right + near_left2 + own + from_left
    sums = [
        jnp.sum(residual * residual, axis=1),
        jnp.sum(direction * gp_image, axis=1),
        jnp.sum(residual * gp_image, axis=1),
        jnp.sum(gp_image * gp_image, axis=1),
    ]
    sums = total(jnp.concatenate(sums)).reshape(4, rhs)
    old_norm, curvature, mixed, image_norm = sums[0], sums[1], sums[2], sums[3]
    step_size = old_norm / curvature
    new_norm = jnp.maximum(old_norm + step_size * (step_size * image_norm - 2.0 * mixed), 0.0)
    new_solution = solution + step_size[:, None] * direction
    new_residual = residual - step_size[:, None] * gp_image
    new_direction = new_residual + (new_norm / old_norm)[:, None] * direction
    return (new_solution, new_residual, new_direction)


def solution(mesh):
    devices = mesh.devices.reshape(-1)
    low = 32
    split = Mesh(devices.reshape(devices.size // low, low), AXES)
    columns = P(None, AXES)
    return jax.shard_map(
        local,
        mesh=split,
        in_specs=(columns, P(), P(AXES), columns, columns, columns),
        out_specs=(columns, columns, columns),
        check_vma=False,
    )
```

```python
import functools
import math

import jax
import jax.numpy as jnp
from jax import lax
from jax.experimental import pallas as pl
from jax.experimental.pallas import tpu as pltpu
from jax.sharding import Mesh, PartitionSpec as P

ROUNDS = 3
TILE = 256
AXES = ("hi", "lo")
VMEM_LIMIT = 40 * 1024 * 1024

LN2 = math.log(2.0)
COORD_SCALE = math.sqrt(5.0) / LN2
SCALE = LN2 * LN2 / 3.0
LINEAR = 3.0 / LN2
CONSTANT = 1.0 / SCALE
TINY = 1e-30

bf16 = jnp.bfloat16
f32 = jnp.float32


def split2(value):
    high = value.astype(bf16)
    return high, (value - high.astype(f32)).astype(bf16)


def split3(value):
    high = value.astype(bf16).astype(f32)
    rest = value - high
    middle = rest.astype(bf16).astype(f32)
    low = (rest - middle).astype(bf16).astype(f32)
    return high, middle, low


def stacked(value):
    return jnp.concatenate(split2(value), axis=0)


def features(scaled, left):
    high, middle, low = split3(-2.0 * scaled if left else scaled)
    norm = split3(jnp.sum(scaled * scaled, axis=0, keepdims=True))
    row = lax.broadcasted_iota(jnp.int32, scaled.shape, 0)
    first = 0 if left else 3
    extra = jnp.where((row >= 3 - first) & (row < 6 - first), 1.0, 0.0)
    for place, part in enumerate(norm):
        extra = jnp.where(row == first + place, part, extra)
    zero = jnp.zeros_like(extra)
    if left:
        pieces = (high, high, middle, high, middle, low, extra, zero)
    else:
        pieces = (high, middle, high, low, middle, high, extra, zero)
    return jnp.concatenate(pieces, axis=0)


def covariance(squared):
    squared = jnp.maximum(squared, TINY)
    less = -squared * lax.rsqrt(squared)
    return ((squared + CONSTANT) - LINEAR * less) * jnp.exp2(less)


def product(left, right):
    return jnp.dot(left, right, preferred_element_type=f32)


def product_t(left, right):
    return lax.dot_general(left, right, (((1,), (1,)), ((), ())), preferred_element_type=f32)


def applied(dot, sides, high, low):
    rows = sides.shape[0] // 2
    both = dot(sides, high)
    return both[:rows] + both[rows:] + dot(sides[:rows], low)


def left_side(packed_ref, inv_ref):
    scaled = packed_ref[0:8, :] * (inv_ref[...] * COORD_SCALE)
    return features(scaled, True).T.astype(bf16), stacked(packed_ref[8:24, :] * SCALE)


def right_side(packed_ref, inv_ref):
    scaled = packed_ref[0:8, :] * (inv_ref[...] * COORD_SCALE)
    return features(scaled, False).astype(bf16), stacked(packed_ref[8:24, :] * SCALE)


def prepare_body(packed_ref, inv_ref, left_ref, sides_ref):
    left_ref[...], sides_ref[...] = left_side(packed_ref, inv_ref)


def block_products(left, sides, far_ref, inv_ref, base_ref, near_ref, back_ref):
    sites = far_ref.shape[1]
    right, far_sides = right_side(far_ref, inv_ref)
    near = None
    for start in range(0, sites, TILE):
        columns = slice(start, start + TILE)
        values = covariance(product(left, right[:, columns]))
        high, low = split2(values)
        part = applied(product_t, far_sides[:, columns], high, low)
        near = part if near is None else near + part
        back = applied(product, sides, high, low)
        back_ref[:, columns] = back if base_ref is None else back + base_ref[:, columns]
    near_ref[...] = near


def own_pair_body(left_ref, sides_ref, far_ref, inv_ref, base_ref, near_ref, back_ref):
    block_products(left_ref[...], sides_ref[...], far_ref, inv_ref, base_ref, near_ref, back_ref)


def first_pair_body(left_ref, sides_ref, far_ref, inv_ref, near_base_ref, near_ref, back_ref):
    block_products(left_ref[...], sides_ref[...], far_ref, inv_ref, None, near_ref, back_ref)
    near_ref[...] += near_base_ref[...]


def far_pair_body(one_ref, other_ref, inv_ref, base_ref, near_ref, back_ref):
    left, sides = left_side(one_ref, inv_ref)
    block_products(left, sides, other_ref, inv_ref, base_ref, near_ref, back_ref)


def self_body(tiles, left_ref, sides_ref, own_ref, inv_ref, *refs):
    out_ref = refs[-1]
    right, _ = right_side(own_ref, inv_ref)
    out_ref[...] = jnp.zeros_like(out_ref)
    for tile in tiles:
        start, stop = tile * TILE, (tile + 1) * TILE
        columns = slice(start, stop)
        values = covariance(product(left_ref[0:stop, :], right[:, columns]))
        high, low = split2(values)
        out_ref[:, 0:stop] += applied(product_t, sides_ref[:, columns], high, low)
        if start:
            out_ref[:, columns] += applied(product, sides_ref[:, 0:start], high[0:start], low[0:start])
    out = (2.0 * ROUNDS) * out_ref[...]
    out_ref[...] = out + refs[0][...] if len(refs) == 2 else out


def call(body, name, shapes, cost):
    return pl.pallas_call(
        body,
        out_shape=shapes,
        compiler_params=pltpu.CompilerParams(vmem_limit_bytes=VMEM_LIMIT),
        cost_estimate=pl.CostEstimate(flops=cost, bytes_accessed=600000, transcendentals=0),
        name=name,
    )


def shape(rows, columns, dtype=f32):
    return jax.ShapeDtypeStruct((rows, columns), dtype)


def prepare(packed, inv):
    rows, sites = packed.shape
    shapes = (shape(sites, 64, bf16), shape(2 * (rows - 8), sites, bf16))
    return call(prepare_body, "prepare", shapes, 10**7)(packed, inv)


def own_pair(left, sides, far, inv, base):
    out = shape(16, far.shape[1])
    return call(own_pair_body, "own_pair", (out, out), 6 * 10**9)(left, sides, far, inv, base)


def first_pair(left, sides, far, inv, near_base):
    out = shape(16, far.shape[1])
    return call(first_pair_body, "first_pair", (out, out), 6 * 10**9)(left, sides, far, inv, near_base)


def far_pair(one, other, inv, base):
    out = shape(16, one.shape[1])
    return call(far_pair_body, "far_pair", (out, out), 6 * 10**9)(one, other, inv, base)


def own_block(tiles, left, sides, packed, inv, *base):
    body = functools.partial(self_body, tiles)
    return call(body, "own", shape(16, packed.shape[1]), 2 * 10**9)(left, sides, packed, inv, *base)


def shifted(value, steps):
    count = lax.axis_size(AXES)
    pairs = [(source, (source + steps) % count) for source in range(count)]
    return lax.ppermute(value, AXES, pairs)


def total(values):
    for axis in ("lo", "hi"):
        count = lax.axis_size(axis)
        copies = jnp.broadcast_to(values[None], (count,) + values.shape)
        values = jnp.sum(lax.all_to_all(copies, axis, 0, 0, tiled=True), axis=0)
    return values


def local(coords, inv_scale, noise_var, solution, residual, direction):
    rhs = direction.shape[0]
    packed = jnp.concatenate([coords, direction], axis=0)
    inv = inv_scale[:, None]
    left2 = shifted(packed, 2)
    right = shifted(packed, -1)
    left, sides = prepare(packed, inv)
    count = packed.shape[1] // TILE
    early = count // 2
    own_early = own_block(range(early), left, sides, packed, inv)
    near_left2, to_left2 = first_pair(left, sides, left2, inv, own_early)
    to_right, to_left2 = far_pair(right, left2, inv, to_left2)
    from_right2 = shifted(to_left2, -2)
    near_right, to_right = own_pair(left, sides, right, inv, to_right)
    from_left = shifted(to_right, 1)
    own = own_block(range(early, count), left, sides, packed, inv, from_right2)
    gp_image = noise_var[None, :] * direction + near_right + near_left2 + own + from_left
    sums = [
        jnp.sum(residual * residual, axis=1),
        jnp.sum(direction * gp_image, axis=1),
        jnp.sum(residual * gp_image, axis=1),
        jnp.sum(gp_image * gp_image, axis=1),
    ]
    sums = total(jnp.concatenate(sums)).reshape(4, rhs)
    old_norm, curvature, mixed, image_norm = sums[0], sums[1], sums[2], sums[3]
    step_size = old_norm / curvature
    new_norm = jnp.maximum(old_norm + step_size * (step_size * image_norm - 2.0 * mixed), 0.0)
    new_solution = solution + step_size[:, None] * direction
    new_residual = residual - step_size[:, None] * gp_image
    new_direction = new_residual + (new_norm / old_norm)[:, None] * direction
    return (new_solution, new_residual, new_direction)


def solution(mesh):
    devices = mesh.devices.reshape(-1)
    low = 32
    split = Mesh(devices.reshape(devices.size // low, low), AXES)
    columns = P(None, AXES)
    return jax.shard_map(
        local,
        mesh=split,
        in_specs=(columns, P(), P(AXES), columns, columns, columns),
        out_specs=(columns, columns, columns),
        check_vma=False,
    )
```

```python
import functools
import math

import jax
import jax.numpy as jnp
from jax import lax
from jax.experimental import pallas as pl
from jax.experimental.pallas import tpu as pltpu
from jax.sharding import Mesh, PartitionSpec as P

ROUNDS = 3
TILE = 256
AXES = ("hi", "ring", "core")
VMEM_LIMIT = 40 * 1024 * 1024

LN2 = math.log(2.0)
COORD_SCALE = math.sqrt(5.0) / LN2
SCALE = LN2 * LN2 / 3.0
LINEAR = 3.0 / LN2
CONSTANT = 1.0 / SCALE
TINY = 1e-30

bf16 = jnp.bfloat16
f32 = jnp.float32


def split2(value):
    high = value.astype(bf16)
    return high, (value - high.astype(f32)).astype(bf16)


def split3(value):
    high = value.astype(bf16).astype(f32)
    rest = value - high
    middle = rest.astype(bf16).astype(f32)
    low = (rest - middle).astype(bf16).astype(f32)
    return high, middle, low


def stacked(value):
    return jnp.concatenate(split2(value), axis=0)


def features(scaled, left):
    high, middle, low = split3(-2.0 * scaled if left else scaled)
    norm = split3(jnp.sum(scaled * scaled, axis=0, keepdims=True))
    row = lax.broadcasted_iota(jnp.int32, scaled.shape, 0)
    first = 0 if left else 3
    extra = jnp.where((row >= 3 - first) & (row < 6 - first), 1.0, 0.0)
    for place, part in enumerate(norm):
        extra = jnp.where(row == first + place, part, extra)
    zero = jnp.zeros_like(extra)
    if left:
        pieces = (high, high, middle, high, middle, low, extra, zero)
    else:
        pieces = (high, middle, high, low, middle, high, extra, zero)
    return jnp.concatenate(pieces, axis=0)


def covariance(squared):
    squared = jnp.maximum(squared, TINY)
    less = -squared * lax.rsqrt(squared)
    return ((squared + CONSTANT) - LINEAR * less) * jnp.exp2(less)


def product(left, right):
    return jnp.dot(left, right, preferred_element_type=f32)


def product_t(left, right):
    return lax.dot_general(left, right, (((1,), (1,)), ((), ())), preferred_element_type=f32)


def applied(dot, sides, high, low):
    rows = sides.shape[0] // 2
    both = dot(sides, high)
    return both[:rows] + both[rows:] + dot(sides[:rows], low)


def left_side(packed_ref, inv_ref):
    scaled = packed_ref[0:8, :] * (inv_ref[...] * COORD_SCALE)
    return features(scaled, True).T.astype(bf16), stacked(packed_ref[8:24, :] * SCALE)


def right_side(packed_ref, inv_ref):
    scaled = packed_ref[0:8, :] * (inv_ref[...] * COORD_SCALE)
    return features(scaled, False).astype(bf16), stacked(packed_ref[8:24, :] * SCALE)


def prepare_body(packed_ref, inv_ref, left_ref, sides_ref):
    left_ref[...], sides_ref[...] = left_side(packed_ref, inv_ref)


def block_products(left, sides, far_ref, inv_ref, base_ref, near_ref, back_ref):
    sites = far_ref.shape[1]
    right, far_sides = right_side(far_ref, inv_ref)
    near = None
    for start in range(0, sites, TILE):
        columns = slice(start, start + TILE)
        values = covariance(product(left, right[:, columns]))
        high, low = split2(values)
        part = applied(product_t, far_sides[:, columns], high, low)
        near = part if near is None else near + part
        back = applied(product, sides, high, low)
        back_ref[:, columns] = back if base_ref is None else back + base_ref[:, columns]
    near_ref[...] = near


def own_pair_body(left_ref, sides_ref, far_ref, inv_ref, base_ref, near_ref, back_ref):
    block_products(left_ref[...], sides_ref[...], far_ref, inv_ref, base_ref, near_ref, back_ref)


def first_pair_body(left_ref, sides_ref, far_ref, inv_ref, near_base_ref, near_ref, back_ref):
    block_products(left_ref[...], sides_ref[...], far_ref, inv_ref, None, near_ref, back_ref)
    near_ref[...] += near_base_ref[...]


def far_pair_body(one_ref, other_ref, inv_ref, base_ref, near_ref, back_ref):
    left, sides = left_side(one_ref, inv_ref)
    block_products(left, sides, other_ref, inv_ref, base_ref, near_ref, back_ref)


def self_body(tiles, left_ref, sides_ref, own_ref, inv_ref, *refs):
    out_ref = refs[-1]
    right, _ = right_side(own_ref, inv_ref)
    out_ref[...] = jnp.zeros_like(out_ref)
    for tile in tiles:
        start, stop = tile * TILE, (tile + 1) * TILE
        columns = slice(start, stop)
        values = covariance(product(left_ref[0:stop, :], right[:, columns]))
        high, low = split2(values)
        out_ref[:, 0:stop] += applied(product_t, sides_ref[:, columns], high, low)
        if start:
            out_ref[:, columns] += applied(product, sides_ref[:, 0:start], high[0:start], low[0:start])
    out = (2.0 * ROUNDS) * out_ref[...]
    out_ref[...] = out + refs[0][...] if len(refs) == 2 else out


def call(body, name, shapes, cost):
    return pl.pallas_call(
        body,
        out_shape=shapes,
        compiler_params=pltpu.CompilerParams(vmem_limit_bytes=VMEM_LIMIT),
        cost_estimate=pl.CostEstimate(flops=cost, bytes_accessed=600000, transcendentals=0),
        name=name,
    )


def shape(rows, columns, dtype=f32):
    return jax.ShapeDtypeStruct((rows, columns), dtype)


def prepare(packed, inv):
    rows, sites = packed.shape
    shapes = (shape(sites, 64, bf16), shape(2 * (rows - 8), sites, bf16))
    return call(prepare_body, "prepare", shapes, 10**7)(packed, inv)


def own_pair(left, sides, far, inv, base):
    out = shape(16, far.shape[1])
    return call(own_pair_body, "own_pair", (out, out), 6 * 10**9)(left, sides, far, inv, base)


def first_pair(left, sides, far, inv, near_base):
    out = shape(16, far.shape[1])
    return call(first_pair_body, "first_pair", (out, out), 6 * 10**9)(left, sides, far, inv, near_base)


def far_pair(one, other, inv, base):
    out = shape(16, one.shape[1])
    return call(far_pair_body, "far_pair", (out, out), 6 * 10**9)(one, other, inv, base)


def own_block(tiles, left, sides, packed, inv, *base):
    body = functools.partial(self_body, tiles)
    return call(body, "own", shape(16, packed.shape[1]), 2 * 10**9)(left, sides, packed, inv, *base)


def shifted(value, steps):
    count = lax.axis_size(AXES)
    pairs = [(source, (source + steps) % count) for source in range(count)]
    return lax.ppermute(value, AXES, pairs)


def total(values):
    for axis in (("ring",), ("hi", "core")):
        count = lax.axis_size(axis)
        copies = jnp.broadcast_to(values[None], (count,) + values.shape)
        values = jnp.sum(lax.all_to_all(copies, axis, 0, 0, tiled=True), axis=0)
    return values


def local(coords, inv_scale, noise_var, solution, residual, direction):
    rhs = direction.shape[0]
    packed = jnp.concatenate([coords, direction], axis=0)
    inv = inv_scale[:, None]
    left2 = shifted(packed, 2)
    right = shifted(packed, -1)
    left, sides = prepare(packed, inv)
    count = packed.shape[1] // TILE
    early = count // 2
    own_early = own_block(range(early), left, sides, packed, inv)
    near_left2, to_left2 = first_pair(left, sides, left2, inv, own_early)
    to_right, to_left2 = far_pair(right, left2, inv, to_left2)
    from_right2 = shifted(to_left2, -2)
    near_right, to_right = own_pair(left, sides, right, inv, to_right)
    from_left = shifted(to_right, 1)
    own = own_block(range(early, count), left, sides, packed, inv, from_right2)
    gp_image = noise_var[None, :] * direction + near_right + near_left2 + own + from_left
    sums = [
        jnp.sum(residual * residual, axis=1),
        jnp.sum(direction * gp_image, axis=1),
        jnp.sum(residual * gp_image, axis=1),
        jnp.sum(gp_image * gp_image, axis=1),
    ]
    sums = total(jnp.concatenate(sums)).reshape(4, rhs)
    old_norm, curvature, mixed, image_norm = sums[0], sums[1], sums[2], sums[3]
    step_size = old_norm / curvature
    new_norm = jnp.maximum(old_norm + step_size * (step_size * image_norm - 2.0 * mixed), 0.0)
    new_solution = solution + step_size[:, None] * direction
    new_residual = residual - step_size[:, None] * gp_image
    new_direction = new_residual + (new_norm / old_norm)[:, None] * direction
    return (new_solution, new_residual, new_direction)


def solution(mesh):
    devices = mesh.devices.reshape(-1)
    split = Mesh(devices.reshape(devices.size // 32, 16, 2), AXES)
    columns = P(None, AXES)
    return jax.shard_map(
        local,
        mesh=split,
        in_specs=(columns, P(), P(AXES), columns, columns, columns),
        out_specs=(columns, columns, columns),
        check_vma=False,
    )
```
